128 devices in a mesh: lon: 32 (over z, x, y_hi), lat: 4 (over y_lo, core).
Axes of the slice: x: 4, y: 4 (y_hi: 2, y_lo: 2; y = y_hi * 2 + y_lo), z: 4, core: 2. Of those that a mesh axis runs over, the one named last changes fastest.
Arguments:
- kappa_east: float32 [64, 4096], P('lat', 'lon'), may hold values from 0.02 to 0.2
- kappa_north: float32 [64, 4096], P('lat', 'lon'), may hold values from 0.02 to 0.2
- depth: int32 [64, 4096], P('lat', 'lon'), may hold values from 0 to 75
- sigma: float32 [151], replicated, may hold values from 0.3 to 3
- obs_precision: float32 [151], replicated, may hold values from 0.5 to 4
- obs_tile: int32 [16384, 1], P(('lon', 'lat')), may hold values from 0 to 31; in each aligned block of 128 rows (0 to 127, 128 to 255, ...) at most 8 rows name the same one
- obs_col: int32 [16384], P(('lon', 'lat')), may hold values from 0 to 127
- obs_lat: int32 [16384], P(('lon', 'lat')), may hold values from 0 to 15
- innovation: float32 [151, 16384], P(None, ('lon', 'lat')), may hold values from -6 to 6
Outputs:
- increment: float32 [151, 64, 4096], P(None, 'lat', 'lon')
- residual: float32 [151, 64, 4096], P(None, 'lat', 'lon')
The draws below stay inside these ranges and needn't reach their ends.
Inputs may be any that keep to these rules, and one draw needn't show every extreme that they name: `obs_tile`: among the 128 profiles listed on one device, no longitude tile is named by more than 8, a bound that some block reaches.
All inputs are finite; a program needn't handle non-finite values.
Results may differ from the reference program's by a relative error of at most 0.00013.
Values sent between devices are 32-bit elements; how exact they have to be, the bound alone decides.
No kernel may reach another device: no remote copies, remote signals or barrier semaphores. Data moves between devices by JAX's collectives and lax.ppermute only.
A program may use at most 128 MiB of HBM per device.

```python
import math
import jax
import jax.numpy as jnp
import numpy as np

NZ = 75
CX = 128
CY = 16
OBS_DEV = 128
ITERS = 2
CH = 151
NX = 4096
NY = 64
NOBS = 16384
CAP = 8
N_LON = 32
N_LAT = 4


def set_ends(values, own_key, least, largest):
    longest = values.shape.index(max(values.shape))
    spots = []
    for shift in (0, 1):
        where = [jax.random.randint(jax.random.fold_in(own_key, axis), (), 0, length) for axis, length in enumerate(values.shape)]
        where[longest] = (where[longest] + shift) % values.shape[longest]
        spots.append(tuple(where))
    return values.at[spots[0]].set(least).at[spots[1]].set(largest)


def shard_levels(key, shape, shards, smallest, top_value):
    level, own = 1.0, jax.random.fold_in(key, 6)
    for dim, shards_of in shards:
        draws = jnp.exp(jax.random.uniform(jax.random.fold_in(own, dim), (shards_of,), jnp.float32, smallest / len(shards), top_value / len(shards)))
        level = level * jnp.repeat(draws, shape[dim] // shards_of).reshape([-1 if axis == dim else 1 for axis in range(len(shape))])
    return level


def routed_block(key, own, number, rows, amount, top, limit, skew):
    ranking = jax.random.permutation(key, amount)
    heavy_load, common = load_shares(amount, rows * top, limit, skew, True), load_shares(amount, rows * top, limit, skew, False)
    places = jnp.arange(amount)

    def named(lengths, offset_by):
        used = int((lengths > 0).sum())
        fixed = max(1, used // 4)
        shifted = fixed + (places - fixed + offset_by * (used - fixed)) % max(1, amount - fixed)
        return jnp.zeros((amount,), jnp.int32).at[ranking[jnp.where(places < fixed, places, shifted)]].set(jnp.asarray(lengths, jnp.int32))

    lengths = jnp.where(number % 4 == 0, named(heavy_load, number // 4), named(common, number - number // 4 - 1))
    mixed = jax.random.permutation(jax.random.fold_in(own, 3), amount)
    donor, receiver = mixed[0:amount // 2 * 2:2], mixed[1:amount // 2 * 2:2]
    room = jnp.minimum(lengths[donor] - 1, limit - lengths[receiver]) // 2
    room = jnp.where((donor == ranking[0]) | (receiver == ranking[0]) | (lengths[receiver] == 0), 0, jnp.maximum(room, 0))
    shifted = jax.random.randint(jax.random.fold_in(own, 4), (amount // 2,), 0, 1 << 20) % (room + 1)
    lengths = lengths.at[donor].add(-shifted).at[receiver].add(shifted)
    labels = jnp.searchsorted(jnp.cumsum(lengths), jnp.arange(rows * top), side="right").astype(jnp.int32)
    listing = labels.reshape(top, rows).T
    listing = listing[jax.random.permutation(jax.random.fold_in(own, 1), rows)]
    offset_by = jax.random.randint(jax.random.fold_in(own, 2), (rows, 1), 0, top)
    return jnp.take_along_axis(listing, (jnp.arange(top)[None, :] + offset_by) % top, axis=1)


def load_shares(count, total, limit, skew, full):
    weights = [(1 << 20) // math.isqrt(standing ** skew) + 1 for standing in range(1, count + 1)]
    largest = limit if full else min(limit, max(-(-total // count), total * weights[0] // sum(weights)))
    least = 1 if total - largest >= count - 1 else 0
    holding, surplus = [largest] + [least] * (count - 1), total - largest - least * (count - 1)
    while surplus > 0:
        movable = [i for i in range(1, count) if holding[i] < largest] or [i for i in range(1, count) if holding[i] < limit]
        whole, budget = sum([weights[i] for i in movable]), surplus
        for i in movable:
            more = min(limit - holding[i], max(1, budget * weights[i] // whole), surplus)
            holding[i] = holding[i] + more
            surplus = surplus - more
    return np.array(holding)


def scatter_about(stream_key, shape, spread, reach, shards=(), kind=jnp.bfloat16):
    array = spread * jax.random.normal(stream_key, shape, jnp.float32)
    if shards:
        array = array * shard_levels(stream_key, shape, shards, -0.22, 0.18)
    return jnp.clip(array, -reach, reach).astype(kind)


def setup_inputs(seed: int = 0) -> dict:
    seeds = jax.random.split(jax.random.key(seed), 10)
    kappa_east = jnp.clip(0.02 + 0.18 * jax.random.uniform(seeds[0], (NY, NX), jnp.float32) ** shard_levels(seeds[0], (NY, NX), ((0, 4), (1, 32)), -0.2, 0.2), 0.02, 0.2)
    kappa_north = jnp.clip(0.02 + 0.18 * jax.random.uniform(seeds[1], (NY, NX), jnp.float32) ** shard_levels(seeds[1], (NY, NX), ((0, 4), (1, 32)), -0.2, 0.2), 0.02, 0.2)
    depth = set_ends(jax.random.randint(seeds[2], (NY, NX), 0, NZ + 1), jax.random.fold_in(seeds[2], 1), 0, NZ).astype(jnp.int32)
    sigma = jnp.clip(jnp.exp(jax.random.uniform(seeds[3], (CH,), jnp.float32, math.log(0.3), math.log(3.0))), 0.3, 3.0)
    obs_precision = jnp.clip(jnp.exp(jax.random.uniform(seeds[4], (CH,), jnp.float32, math.log(0.5), math.log(4.0))), 0.5, 4.0)
    obs_tile_keys = jax.random.split(jax.random.fold_in(seeds[5], 1), NOBS // OBS_DEV)
    obs_tile_turns = jax.random.permutation(jax.random.fold_in(seeds[5], 3), NOBS // OBS_DEV)
    obs_tile = jax.vmap(lambda own, number: routed_block(jax.random.fold_in(seeds[5], 2), own, number, OBS_DEV, N_LON, 1, CAP, 0))(obs_tile_keys, obs_tile_turns).reshape((NOBS, 1))
    obs_col = set_ends(jax.random.randint(seeds[6], (NOBS,), 0, CX), jax.random.fold_in(seeds[6], 1), 0, CX - 1).astype(jnp.int32)
    obs_lat = set_ends(jax.random.randint(seeds[7], (NOBS,), 0, CY), jax.random.fold_in(seeds[7], 1), 0, CY - 1).astype(jnp.int32)
    innovation = scatter_about(seeds[8], (CH, NOBS), 1.0, 6.0, ((1, 128),), jnp.float32)
    return dict(kappa_east=kappa_east, kappa_north=kappa_north, depth=depth, sigma=sigma, obs_precision=obs_precision, obs_tile=obs_tile, obs_col=obs_col, obs_lat=obs_lat, innovation=innovation)


def smooth_once(v, face_east, face_north):
    east = jnp.roll(v, -1, 2)
    west = jnp.roll(v, 1, 2)
    north = jnp.roll(v, -1, 1)
    south = jnp.roll(v, 1, 1)
    out = v + face_east * (east - v) + jnp.roll(face_east, 1, 2) * (west - v)
    return out + face_north * (north - v) + jnp.roll(face_north, 1, 1) * (south - v)


def smooth_five(v, face_east, face_north):
    for step in range(5):
        v = smooth_once(v, face_east, face_north)
    return v


def reference(kappa_east, kappa_north, depth, sigma, obs_precision, obs_tile, obs_col, obs_lat, innovation):
    levels = jnp.arange(CH, dtype=jnp.int32)
    level_of = jnp.where(levels < 2 * NZ, levels % NZ, 0).astype(jnp.int32)
    wet = (depth[None, :, :] > level_of[:, None, None]).astype(jnp.float32)
    keep_row = (jnp.arange(NY, dtype=jnp.int32) < NY - 1).astype(jnp.float32)[:, None]
    face_east = kappa_east[None] * wet * jnp.roll(wet, -1, 2)
    face_north = (kappa_north * keep_row)[None] * wet * jnp.roll(wet, -1, 1)
    order = jnp.arange(NOBS, dtype=jnp.int32)
    obs_row = ((order // OBS_DEV) % N_LAT) * CY + obs_lat
    obs_lon = (obs_tile[:, 0] * CX + obs_col).astype(jnp.int32)
    scale = sigma[:, None, None]
    weight = obs_precision[:, None]

    def forward_obs(u):
        return (u * wet)[:, obs_row, obs_lon]

    def adjoint_obs(w):
        cells = jnp.zeros((CH, NY, NX), jnp.float32).at[:, obs_row, obs_lon].add(w)
        return cells * wet

    def hessian(p):
        u = scale * smooth_five(p, face_east, face_north)
        w = weight * forward_obs(u)
        return p + smooth_five(scale * adjoint_obs(w), face_east, face_north)

    rhs = smooth_five(scale * adjoint_obs(weight * innovation), face_east, face_north)
    increment = jnp.zeros_like(rhs)
    residual = rhs
    direction = rhs
    norm_now = jnp.sum(residual * residual)
    for step in range(ITERS):
        image = hessian(direction)
        alpha = norm_now / jnp.sum(direction * image)
        increment = increment + alpha * direction
        residual = residual - alpha * image
        norm_next = jnp.sum(residual * residual)
        direction = residual + (norm_next / norm_now) * direction
        norm_now = norm_next
    return increment, residual
```

```python
import jax
import jax.numpy as jnp
from jax import lax
from jax.experimental import pallas as pl
from jax.experimental.pallas import tpu as pltpu
from jax.sharding import PartitionSpec as P

NZ = 75
CAP = 8
HALF = 76
QUART = 38
SLOT = 40
IDX = 80
PAIRS = 5
KINDS = 15
ROWS = 57
DEPTH = 58
LANES = 128
EDGE = 32
BAND = 16
ALL = ("lon", "lat")
VMEM_LIMIT = 60 * 1024 * 1024


def split_parts(x, count):
    parts = []
    for step in range(count):
        part = x.astype(jnp.bfloat16)
        parts.append(part)
        if step + 1 < count:
            x = x - part.astype(jnp.float32)
    return parts


def pack_kernel(tiles, tile_col, tile_row, obs_lat, obs_col, values, out):
    trow = tile_row[...]
    seen = jnp.logical_and(
        tile_col[...] == trow,
        lax.broadcasted_iota(jnp.int32, (LANES, LANES), 0)
        < lax.broadcasted_iota(jnp.int32, (LANES, LANES), 1),
    )
    rank = jnp.sum(jnp.where(seen, 1.0, 0.0), axis=0, keepdims=True).astype(jnp.int32)
    place = (obs_lat[...] * LANES + obs_col[...] + 1).astype(jnp.float32)
    slots = lax.broadcasted_iota(jnp.int32, (tiles * CAP, LANES), 0)
    marks = []
    for shift in (0, 1, tiles - 1):
        at = lax.rem(trow + shift, tiles) * CAP + rank
        marks.append(jnp.where(slots == at, 1.0, 0.0).astype(jnp.bfloat16))
    lines = lax.broadcasted_iota(jnp.int32, (16, LANES), 0)
    for half in range(2):
        vals = values[half]
        blank = jnp.zeros((IDX, LANES), jnp.float32)
        total = None
        for block in range(3):
            pieces = [vals if j == block else blank for j in range(3)]
            pieces.append(jnp.where(lines == block, place, 0.0))
            right = jnp.concatenate(pieces, axis=0)
            for part in split_parts(right, 3):
                term = lax.dot_general(
                    marks[block],
                    part,
                    (((1,), (1,)), ((), ())),
                    preferred_element_type=jnp.float32,
                )
                total = term if total is None else total + term
        cube = total.reshape(tiles, CAP, 256)
        out[:, half] = cube
        out[:, 2 + half] = cube


def main_kernel(where_ref, recv, geo, par, keep, send, sums, V, FE, FN, DC, XM, XP, G2, LEV):
    y = where_ref[0]
    core = where_ref[1]
    r_low = y * 7
    lane = lax.broadcasted_iota(jnp.int32, (8, LANES), 1)
    l127, l63, l0, l64 = lane == 127, lane == 63, lane == 0, lane == 64
    inner = jnp.logical_and(lane >= 32, lane < 96)

    lane2 = lax.broadcasted_iota(jnp.int32, (64, LANES), 1)
    row2 = lax.broadcasted_iota(jnp.int32, (64, LANES), 0)
    d_own, d_rim = geo[2], geo[5]
    d_turn = pltpu.roll(d_own, 64, 1)
    east_own = jnp.where(lane2 == 127, pltpu.roll(d_rim, 127, 1), pltpu.roll(d_own, 127, 1))
    east_rim = jnp.where(
        lane2 == 127,
        pltpu.roll(d_own, 127, 1),
        jnp.where(lane2 == 63, pltpu.roll(d_turn, 127, 1), pltpu.roll(d_rim, 127, 1)),
    )
    for kind, (ke, kn, d, e) in enumerate(
        ((geo[0], geo[1], d_own, east_own), (None, None, None, None), (geo[3], geo[4], d_rim, east_rim))
    ):
        if kind == 1:
            continue
        wall = jnp.where(row2 == 63, 0.0, kn)
        fields = (ke, jnp.minimum(d, e), wall, jnp.minimum(d, pltpu.roll(d, 63, 0)), d)
        for which, field in enumerate(fields):
            G2[kind * 5 + which] = field
            if kind == 0:
                G2[5 + which] = pltpu.roll(field, 64, 1)
    for p in range(PAIRS):
        low = par[0, pl.ds(8 * p, 8), :]
        high = par[0, pl.ds(8 * (p + 5), 8), :]
        LEV[p * 3] = low
        LEV[p * 3 + 1] = high
        LEV[p * 3 + 2] = jnp.where(inner, high, low)

    lanes_a = lax.broadcasted_iota(jnp.int32, (256, 256), 1)
    lanes_b = lax.broadcasted_iota(jnp.int32, (256, LANES), 1)

    def band(k, carry):
        block = recv[:, k].reshape(256, 256)
        turned = block.T
        places = block[:, 240:243].astype(jnp.int32) - 1
        main_col = jnp.bitwise_and(places[:, 0:1], 127)
        left_col = jnp.bitwise_and(places[:, 1:2], 127)
        right_col = jnp.bitwise_and(places[:, 2:3], 127)
        hot_main = jnp.logical_or(
            lanes_a == main_col, lanes_a == 128 + jnp.bitwise_and(main_col + 64, 127)
        )
        left_ok = left_col >= LANES - EDGE
        hot_left = jnp.logical_and(
            left_ok, jnp.logical_or(lanes_b == left_col, lanes_b == left_col - 64)
        )
        right_ok = right_col < EDGE
        hot_right = jnp.logical_and(
            right_ok, jnp.logical_or(lanes_b == right_col, lanes_b == right_col + 64)
        )
        as16 = lambda m: jnp.where(m, 1.0, 0.0).astype(jnp.bfloat16)
        hot_main, hot_left, hot_right = as16(hot_main), as16(hot_left), as16(hot_right)
        rows_at = lax.shift_right_arithmetic(turned[240:248].astype(jnp.int32) - 1, 7)
        totals = []
        for b, hot in ((0, hot_main), (1, hot_left), (2, hot_right)):
            vals = turned[b * IDX : (b + 1) * IDX]
            at = rows_at[b : b + 1]
            acc = None
            for part in split_parts(vals, 3):
                wide = jnp.concatenate(
                    [part * jnp.where(at == i, 1.0, 0.0).astype(jnp.bfloat16) for i in range(BAND)],
                    axis=0,
                )
                term = jnp.dot(wide, hot, preferred_element_type=jnp.float32)
                acc = term if acc is None else acc + term
            totals.append(acc)
        row0 = k * BAND * IDX
        XM[pl.ds(pl.multiple_of(row0, 8), BAND * IDX), :] = totals[0]
        XP[pl.ds(pl.multiple_of(row0, 8), BAND * IDX), :] = totals[1] + totals[2]
        return carry

    lax.fori_loop(0, recv.shape[1], band, 0)

    def at(kind, row):
        return pl.multiple_of((kind * DEPTH + row) * 8, 8)

    def fill(rho, carry):
        row = rho + r_low
        base = row * IDX

        def tile(ref, t, off):
            return ref[pl.ds(pl.multiple_of(base + 8 * t, 8), 8), off : off + LANES]

        counts = (
            jnp.broadcast_to(tile(XM, 4, 0)[7:8], (8, LANES)),
            jnp.broadcast_to(tile(XM, 9, 128)[7:8], (8, LANES)),
            jnp.broadcast_to(jnp.where(inner, tile(XP, 9, 0), tile(XP, 4, 0))[7:8], (8, LANES)),
        )
        line = [[G2[k * 5 + f, pl.ds(row, 1), :] for f in range(5)] for k in range(3)]
        for p in range(PAIRS):
            raw = (
                tile(XM, p, 0),
                tile(XM, p + 5, 128),
                jnp.where(inner, tile(XP, p + 5, 0), tile(XP, p, 0)),
            )
            w_low, w_high = par[1, pl.ds(8 * p, 8), :], par[1, pl.ds(8 * (p + 5), 8), :]
            s_low, s_high = par[2, pl.ds(8 * p, 8), :], par[2, pl.ds(8 * (p + 5), 8), :]
            w = (w_low, w_high, jnp.where(inner, w_high, w_low))
            s = (s_low, s_high, jnp.where(inner, s_high, s_low))
            for k in range(3):
                lev = LEV[p * 3 + k]
                ke, de, kn, dn, d = line[k]
                where = pl.ds(at(p * 3 + k, rho), 8)
                FE[where, :] = jnp.where(de > lev, ke, 0.0)
                FN[where, :] = jnp.where(dn > lev, kn, 0.0)
                wet = d > lev
                V[where, :] = jnp.where(wet, raw[k] * w[k], 0.0)
                DC[where, :] = jnp.where(wet, counts[k] * s[k], 0.0)
        return carry

    lax.fori_loop(0, ROWS, fill, 0)
    for kind in range(KINDS):
        V[pl.ds((kind * DEPTH + ROWS) * 8, 8), :] = jnp.zeros((8, LANES), jnp.float32)

    def smooth(start, rows):
        def one(step, carry):
            p = lax.rem(step, PAIRS)
            v = [V[pl.ds(at(p * 3 + k, start), 8), :] for k in range(3)]
            gone = [None, None, None]
            for i in range(rows):
                here = [pl.ds(at(p * 3 + k, start + i), 8) for k in range(3)]
                north = [V[pl.ds(at(p * 3 + k, start + i + 1), 8), :] for k in range(3)]
                t = [pltpu.roll(x, 127, 1) for x in v]
                e = (
                    jnp.where(l127, t[2], t[0]),
                    jnp.where(l63, t[2], t[1]),
                    jnp.where(l127, t[0], jnp.where(l63, t[1], t[2])),
                )
                flux = [FE[here[k], :] * (e[k] - v[k]) for k in range(3)]
                u = [pltpu.roll(x, 1, 1) for x in flux]
                west = (
                    jnp.where(l0, u[2], u[0]),
                    jnp.where(l64, u[2], u[1]),
                    jnp.where(l0, u[0], jnp.where(l64, u[1], u[2])),
                )
                rise = [FN[here[k], :] * (north[k] - v[k]) for k in range(3)]
                for k in range(3):
                    out = (v[k] + flux[k]) - west[k] + rise[k]
                    if gone[k] is not None:
                        out = out - gone[k]
                    V[here[k], :] = out
                v, gone = north, rise
            return carry

        lax.fori_loop(0, 5 * PAIRS, one, 0)

    def weigh(start, rows):
        def one(j, carry):
            for kind in range(KINDS):
                here = pl.ds(at(kind, start + j), 8)
                V[here, :] = V[here, :] * DC[here, :]
            return carry

        lax.fori_loop(0, rows, one, 0)

    def store(which):
        for target, tile_row in ((keep, core), (send, 1 - core)):
            low = 25 * y + 16 * tile_row
            for kind in range(2):

                def one(p, carry):
                    for s in range(8):
                        for j in range(2):
                            src = (((p * 3 + kind) * DEPTH) + low + 8 * j) * 8 + s
                            x = V[pl.ds(src, 8, stride=8), :]
                            if kind == 1:
                                x = pltpu.roll(x, 64, 1)
                            target[which, SLOT * kind + 8 * p + s, 8 * j : 8 * j + 8, :] = x
                    return carry

                lax.fori_loop(0, PAIRS, one, 0)

    smooth(y * 0, 57)
    store(0)
    smooth(y * 5, 52)
    weigh(y * 10, 47)
    smooth(y * 10, 47)
    store(1)
    smooth(y * 15, 42)
    weigh(y * 20, 37)
    smooth(y * 20, 37)
    store(2)

    zero = jnp.zeros((8, LANES), jnp.float32)

    def whole(x):
        return jnp.sum(jnp.sum(x, axis=1, keepdims=True), axis=0, keepdims=True)

    def first(i, acc):
        bb, bm = acc
        for ref in (keep, send):
            for j in range(2):
                here = slice(8 * j, 8 * j + 8)
                b, m = ref[0, i, here, :], ref[1, i, here, :]
                bb, bm = bb + b * b, bm + b * m
        return bb, bm

    bb, bm = (whole(x) for x in lax.fori_loop(0, IDX, first, (zero, zero)))
    mu = jnp.where(bb > 0.0, bm / jnp.where(bb > 0.0, bb, 1.0), 0.0)
    mu_all = jnp.broadcast_to(mu, (8, LANES))

    def second(i, acc):
        zz, zy, zm, by, zb = acc
        for ref in (keep, send):
            for j in range(2):
                here = slice(8 * j, 8 * j + 8)
                b, m, n = ref[0, i, here, :], ref[1, i, here, :], ref[2, i, here, :]
                z = m - mu_all * b
                q = n - mu_all * m
                zz, zy, zm = zz + z * z, zy + z * q, zm + z * m
                by, zb = by + b * q, zb + z * b
        return zz, zy, zm, by, zb

    rest = [whole(x) for x in lax.fori_loop(0, IDX, second, (zero,) * 5)]
    lane_row = lax.broadcasted_iota(jnp.int32, (1, LANES), 1)
    packed = jnp.zeros((1, LANES), jnp.float32)
    for j, x in enumerate([bb, bm, mu] + rest):
        packed = jnp.where(lane_row == j, x, packed)
    sums[...] = jnp.broadcast_to(packed, sums.shape)


def last_kernel(where_ref, sums, keep, got, increment, residual):
    core = where_ref[1]
    table = sums[...]

    def col(j):
        return table[:, j : j + 1]

    def total(x):
        return jnp.sum(x, axis=0, keepdims=True)

    bb, bm, mus, zz, zy, zm, by, zb = (col(j) for j in range(8))
    rr = total(bb)
    h = total(bm)
    mu = h / rr
    off = mus - mu
    a1 = rr / (rr + h)
    z_z = total(zz + 2.0 * off * zb + off * off * bb)
    z_m = total(zm + off * bm)
    b_q = total(by + off * bm)
    z_q = total(zy + off * (zm + by) + off * off * bm)
    new = a1 * a1 * z_z
    beta = new / rr
    size = new + beta * beta * rr
    curve = size + a1 * a1 * z_q - a1 * beta * (z_m + b_q) + beta * beta * h
    a2 = new / curve
    spread = lambda x: jnp.broadcast_to(x, (8, LANES))
    mu, a1, a2, beta = spread(mu), spread(a1), spread(a2), spread(beta)

    def write(ref, idx, channel):
        for j in range(2):
            here = slice(8 * j, 8 * j + 8)
            b, m, n = ref[0, idx, here, :], ref[1, idx, here, :], ref[2, idx, here, :]
            r = a1 * (mu * b - m)
            image = a1 * (mu * m - n) + beta * m
            d = r + beta * b
            increment[channel, here, :] = a1 * b + a2 * d
            residual[channel, here, :] = r - a2 * (d + image)

    for ref, half in ((keep, core), (got, 1 - core)):
        for kind in range(2):
            count = QUART if kind == 0 else QUART - half

            def one(i, carry):
                write(ref, SLOT * kind + i, HALF * half + QUART * kind + i)
                return carry

            lax.fori_loop(0, count, one, 0)


def spec(memory_space=pltpu.VMEM):
    return pl.BlockSpec(memory_space=memory_space)


def local(
    kappa_east, kappa_north, depth, sigma, obs_precision, obs_tile, obs_col, obs_lat, innovation
):
    f32 = jnp.float32
    channels = sigma.shape[0]
    lon_tiles = lax.axis_size("lon")
    lat_tiles = lax.axis_size("lat")
    lat_here = lax.axis_index("lat")
    place = jnp.stack([lat_here // 2, lat_here % 2]).astype(jnp.int32)
    core = lat_here % 2

    def halves(x, fill):
        tail = x.shape[1:]
        pad = jnp.zeros((2 * HALF - channels,) + tail, f32)
        ones = jnp.concatenate([jnp.zeros((1,) + tail, f32), jnp.full((1,) + tail, fill, f32)])
        full = jnp.concatenate([x, pad])
        parts = []
        for q in range(4):
            parts += [full[q * QUART : (q + 1) * QUART], ones]
        return jnp.concatenate(parts).reshape((2, IDX) + tail)

    packed = pl.pallas_call(
        lambda *refs: pack_kernel(lon_tiles, *refs),
        out_shape=jax.ShapeDtypeStruct((lon_tiles, lat_tiles, CAP, 256), f32),
        in_specs=[spec()] * 5,
        out_specs=spec(),
        compiler_params=pltpu.CompilerParams(vmem_limit_bytes=VMEM_LIMIT),
        name="pack",
    )(
        obs_tile,
        obs_tile.reshape(1, LANES),
        obs_lat.reshape(1, LANES),
        obs_col.reshape(1, LANES),
        halves(innovation, 1.0),
    )
    recv = lax.all_to_all(
        packed.reshape(lon_tiles * lat_tiles, CAP, 256), ALL, 0, 0, tiled=True
    ).reshape(lon_tiles, lat_tiles, CAP, 256)

    stacked = jnp.stack([kappa_east, kappa_north, depth.astype(f32)])
    count = lon_tiles
    right = lax.ppermute(stacked[:, :, :EDGE], "lon", [((i + 1) % count, i) for i in range(count)])
    left = lax.ppermute(stacked[:, :, -EDGE:], "lon", [(i, (i + 1) % count) for i in range(count)])
    rim = jnp.concatenate([right, left, right, left], axis=2)
    geo = lax.all_gather(jnp.concatenate([stacked, rim]), "lat", axis=1, tiled=True)

    order = jnp.arange(4 * QUART, dtype=jnp.int32)
    level = jnp.where(order < 2 * NZ, order % NZ, 0)
    level = jnp.where(order < channels, level, 1 << 20).astype(f32)
    pads = jnp.zeros((2 * HALF - channels,), f32)
    scale = jnp.concatenate([sigma, pads])
    weight = jnp.concatenate([obs_precision, pads])

    def own(x, fill):
        mine = lax.dynamic_slice_in_dim(x, core * HALF, HALF)
        fills = jnp.full((2,), fill, f32)
        return jnp.concatenate([mine[:QUART], fills, mine[QUART:], fills])

    par = jnp.stack(
        [own(level, float(1 << 20)), own(scale * weight, 0.0), own(scale * scale * weight, 0.0)]
    )
    par = jnp.broadcast_to(par[:, :, None], (3, IDX, LANES))

    tile_shape = jax.ShapeDtypeStruct((3, IDX, BAND, LANES), f32)
    keep, send, sums = pl.pallas_call(
        main_kernel,
        out_shape=(
            tile_shape,
            tile_shape,
            jax.ShapeDtypeStruct((lon_tiles * lat_tiles, LANES), f32),
        ),
        in_specs=[spec(pltpu.SMEM), spec(), spec(), spec()],
        out_specs=(spec(), spec(), spec()),
        scratch_shapes=[
            pltpu.VMEM((KINDS * DEPTH * 8, LANES), f32),
            pltpu.VMEM((KINDS * DEPTH * 8, LANES), f32),
            pltpu.VMEM((KINDS * DEPTH * 8, LANES), f32),
            pltpu.VMEM((KINDS * DEPTH * 8, LANES), f32),
            pltpu.VMEM((64 * IDX, 256), f32),
            pltpu.VMEM((64 * IDX, LANES), f32),
            pltpu.VMEM((KINDS, 64, LANES), f32),
            pltpu.VMEM((KINDS, 8, LANES), f32),
        ],
        compiler_params=pltpu.CompilerParams(vmem_limit_bytes=VMEM_LIMIT),
        name="iterate",
    )(place, recv, geo, par)

    sums = lax.all_to_all(sums, ALL, 0, 0, tiled=True)
    got = lax.ppermute(send, "lat", [(i, i ^ 1) for i in range(lat_tiles)])
    out = jax.ShapeDtypeStruct((channels, BAND, LANES), f32)
    return pl.pallas_call(
        last_kernel,
        out_shape=(out, out),
        in_specs=[spec(pltpu.SMEM), spec(), spec(), spec()],
        out_specs=(spec(), spec()),
        compiler_params=pltpu.CompilerParams(vmem_limit_bytes=VMEM_LIMIT),
        name="combine",
    )(place, sums, keep, got)


def solution(mesh):
    return jax.shard_map(
        local,
        mesh=mesh,
        in_specs=(
            P("lat", "lon"),
            P("lat", "lon"),
            P("lat", "lon"),
            P(),
            P(),
            P(("lon", "lat"), None),
            P(("lon", "lat")),
            P(("lon", "lat")),
            P(None, ("lon", "lat")),
        ),
        out_specs=(P(None, "lat", "lon"), P(None, "lat", "lon")),
        check_vma=False,
    )
```

```python
import jax
import jax.numpy as jnp
from jax import lax
from jax.experimental import pallas as pl
from jax.experimental.pallas import tpu as pltpu
from jax.sharding import PartitionSpec as P

NZ = 75
CAP = 8
HALF = 80
GROUPS = 10
SEGS = 12
STEPS = 15
LEFT = 26
ROWS = 64
NEED = 57
LANES = 128
EDGE = 32
BAND = 16
CHUNK = 8
LINE = STEPS * 8
ALL = ("lon", "lat")
VMEM_LIMIT = 60 * 1024 * 1024


def split_parts(x, count):
    parts = []
    for step in range(count):
        part = x.astype(jnp.bfloat16)
        parts.append(part)
        if step + 1 < count:
            x = x - part.astype(jnp.float32)
    return parts


def iota(shape, axis):
    return lax.broadcasted_iota(jnp.int32, shape, axis)


def by_twelve(x):
    return lax.shift_right_logical(x * 5462, 16)


def by_fifteen(x):
    return lax.shift_right_logical(x * 4370, 16)


def as16(mask):
    return jnp.where(mask, 1.0, 0.0).astype(jnp.bfloat16)


def dot(a, b):
    return jnp.dot(a, b, preferred_element_type=jnp.float32)


def dot_nt(a, b):
    return lax.dot_general(a, b, (((1,), (1,)), ((), ())), preferred_element_type=jnp.float32)


def pack_kernel(tiles, tile_col, tile_row, obs_lat, obs_col, values, out, wide):
    channels = values.shape[0]
    wide[144:160, :] = jnp.zeros((16, LANES), jnp.float32)
    wide[0:channels, :] = values[...]
    trow = tile_row[...]
    seen = jnp.logical_and(
        tile_col[...] == trow, iota((LANES, LANES), 0) < iota((LANES, LANES), 1)
    )
    rank = jnp.sum(jnp.where(seen, 1.0, 0.0), axis=0, keepdims=True).astype(jnp.int32)
    slots = iota((tiles * CAP, LANES), 0)
    lines = iota((16, LANES), 0)
    marks, codes = [], []
    for block, (shift, base) in enumerate(((0, LEFT), (1, LEFT - LANES), (tiles - 1, LEFT + LANES))):
        at = lax.rem(trow + shift, tiles) * CAP + rank
        marks.append(as16(slots == at))
        u = obs_col[...] + base
        seg = by_fifteen(jnp.maximum(u, 0))
        good = jnp.logical_and(u >= 0, u < SEGS * STEPS)
        code = jnp.where(good, obs_lat[...] * STEPS + u - seg * STEPS + 1, 0)
        codes.append(
            jnp.where(
                lines == 2 * block,
                code.astype(jnp.float32),
                jnp.where(lines == 2 * block + 1, seg.astype(jnp.float32), 0.0),
            )
        )
    blank = jnp.zeros((HALF, LANES), jnp.float32)
    for half in range(2):
        vals = wide[half * HALF : (half + 1) * HALF, :]
        total = None
        for block in range(3):
            pieces = [vals if j == block else blank for j in range(3)] + [codes[block]]
            for part in split_parts(jnp.concatenate(pieces, axis=0), 3):
                term = dot_nt(marks[block], part)
                total = term if total is None else total + term
        cube = total.reshape(tiles, CAP, 256)
        out[:, half] = cube
        out[:, 2 + half] = cube


def main_kernel(where_ref, recv, geo, par, sb, sm, sn, sums, V, W, FE, FN, DC, CNT, G, EXP):
    y = where_ref[0]
    lane = iota((8, LANES), 1)
    seg8 = jnp.where(lane < GROUPS * SEGS, lane - by_twelve(lane) * SEGS, -1)

    own = [geo[f] for f in range(3)]
    both = [jnp.concatenate([geo[f], geo[3 + f]], axis=1) for f in range(3)]
    wide_lane, wide_row = iota((ROWS, 256), 1), iota((ROWS, 256), 0)
    ke, kn, d = both
    kn = jnp.where(wide_row == ROWS - 1, 0.0, kn)
    east = jnp.where(
        wide_lane == LANES + 2 * EDGE - 1,
        jnp.concatenate([pltpu.roll(own[2], 63, 1)] * 2, axis=1),
        pltpu.roll(d, 255, 1),
    )
    fields = (ke, jnp.minimum(d, east), kn, jnp.minimum(d, pltpu.roll(d, ROWS - 1, 0)), d)
    q_lane, q_row = iota((256, LANES), 1), iota((256, LANES), 0)
    q_col = (q_lane - by_twelve(q_lane) * SEGS) * STEPS - LEFT
    parts = [split_parts(x, 3 if f in (0, 2) else 1) for f, x in enumerate(fields)]
    for j in range(STEPS):
        col = q_col + j
        perm = as16(q_row == jnp.where(col < 0, LANES + 2 * EDGE + col, col))
        for f in range(5):
            total = None
            for part in parts[f]:
                term = dot(part, perm)
                total = term if total is None else total + term
            G[f * STEPS + j] = total

    e_lane = iota((256, LANES), 1)
    e_group, e_row = by_twelve(e_lane), iota((256, LANES), 0)
    for g in range(3):
        for s in range(8):
            hit = jnp.logical_and(e_group < GROUPS, e_row == HALF * g + GROUPS * s + e_group)
            EXP[g, :, s * LANES : (s + 1) * LANES] = as16(hit)
        EXP[g, :, 8 * LANES : 9 * LANES] = as16(e_row == 3 * HALF + 2 * g + 1)

    pick = as16(iota((16, 256), 1) == 3 * HALF + iota((16, 256), 0))
    seg_of = jnp.where(e_lane < GROUPS * SEGS, e_lane - e_group * SEGS, -1).astype(jnp.float32)
    cell = (iota((BAND * STEPS, 256), 0) + 1).astype(jnp.float32)

    def band(k, carry):
        hi, mid = split_parts(recv[:, k].reshape(256, 256), 2)
        codes = dot_nt(pick, hi)
        acc, count = None, None
        for g in range(3):
            left = as16(cell == codes[2 * g : 2 * g + 1])
            full = dot(hi, EXP[g])
            rest = dot(mid, EXP[g, :, 0 : 8 * LANES])
            hot = seg_of == full[:, 8 * LANES :]
            for source in (full, rest):
                right = jnp.concatenate(
                    [
                        jnp.where(hot, source[:, s * LANES : (s + 1) * LANES], 0.0).astype(jnp.bfloat16)
                        for s in range(8)
                    ],
                    axis=1,
                )
                term = dot(left, right)
                acc = term if acc is None else acc + term
            term = dot(left, as16(hot))
            count = term if count is None else count + term
        base = k * (BAND * STEPS)
        for s in range(8):
            V[pl.ds(base * 8 + s, BAND * STEPS, stride=8), :] = acc[:, s * LANES : (s + 1) * LANES]
        CNT[pl.ds(pl.multiple_of(base, 8), BAND * STEPS), :] = count
        return carry

    lax.fori_loop(0, recv.shape[1], band, 0)

    def at(row, j):
        return pl.ds(pl.multiple_of(row * LINE + 8 * j, 8), 8)

    level, w_all, s_all = par[0], par[1], par[2]

    def fill(row, carry):
        for j in range(STEPS):
            ke, de, kn, dn, d = [
                G[f * STEPS + j, pl.ds(row, 1), :] for f in range(5)
            ]
            here = at(row, j)
            FE[here, :] = jnp.where(de > level, ke, 0.0)
            FN[here, :] = jnp.where(dn > level, kn, 0.0)
            wet = d > level
            V[here, :] = jnp.where(wet, V[here, :] * w_all, 0.0)
            DC[here, :] = jnp.where(wet, CNT[pl.ds(row * STEPS + j, 1), :] * s_all, 0.0)
        return carry

    lax.fori_loop(0, ROWS, fill, 0)
    for ref in (V, W):
        ref[ROWS * LINE : (ROWS + 1) * LINE, :] = jnp.zeros((LINE, LANES), jnp.float32)

    def sweep(src, dst, number, weighted=False):
        chunks = lax.div(NEED - number + CHUNK - 1, CHUNK)
        start = y * (ROWS - CHUNK * chunks)

        def one(c, carry):
            v, gone = list(carry[:STEPS]), list(carry[STEPS:])
            base = start + c * CHUNK
            for i in range(CHUNK):
                north = [src[at(base + i + 1, j), :] for j in range(STEPS)]
                flux = [None] * STEPS
                last = STEPS - 1
                flux[last] = FE[at(base + i, last), :] * (pltpu.roll(v[0], LANES - 1, 1) - v[last])
                west = pltpu.roll(flux[last], 1, 1)
                for j in range(last):
                    flux[j] = FE[at(base + i, j), :] * (v[j + 1] - v[j])
                for j in list(range(1, STEPS)) + [0]:
                    rise = FN[at(base + i, j), :] * (north[j] - v[j])
                    out = (v[j] + flux[j]) - (flux[j - 1] if j else west) + (rise - gone[j])
                    if weighted:
                        out = out * DC[at(base + i, j), :]
                    dst[at(base + i, j), :] = out
                    gone[j] = rise
                v = north
            return tuple(v) + tuple(gone)

        zero = jnp.zeros((8, LANES), jnp.float32)
        below = jnp.maximum(start - 1, 0)
        v = tuple(src[at(start, j), :] for j in range(STEPS))
        gone = tuple(
            jnp.where(y > 0, FN[at(below, j), :] * (v[j] - src[at(below, j), :]), zero)
            for j in range(STEPS)
        )
        lax.fori_loop(0, chunks, one, v + gone)

    def smooth(src, dst, stage, weighted=False):
        def twice(step, carry):
            number = 5 * stage + 1 + 2 * step
            sweep(src, dst, number)
            sweep(dst, src, number + 1)
            return carry

        lax.fori_loop(0, 2, twice, 0)
        sweep(src, dst, 5 * stage + 5, weighted)

    def save(src, ref):
        def one(i, carry):
            for j in range(STEPS):
                u = seg8 * STEPS + j
                mine = jnp.logical_and(u >= LEFT, u < LEFT + LANES)
                ref[at(i, j), :] = jnp.where(mine, src[at(y * 32 + i, j), :], 0.0)
            return carry

        lax.fori_loop(0, 32, one, 0)

    smooth(V, W, 0)
    save(W, sb)
    smooth(W, V, 1, True)
    smooth(V, W, 2)
    save(W, sm)
    smooth(W, V, 3, True)
    smooth(V, W, 4)
    save(W, sn)

    zero = jnp.zeros((8, LANES), jnp.float32)

    def whole(x):
        return jnp.sum(jnp.sum(x, axis=0, keepdims=True), axis=1, keepdims=True)

    def first(i, acc):
        bb, bm = acc
        for j in range(STEPS):
            b, m = sb[at(i, j), :], sm[at(i, j), :]
            bb, bm = bb + b * b, bm + b * m
        return bb, bm

    bb, bm = (whole(x) for x in lax.fori_loop(0, 32, first, (zero, zero)))
    mu = jnp.where(bb > 0.0, bm / jnp.where(bb > 0.0, bb, 1.0), 0.0)
    mu_all = jnp.broadcast_to(mu, (8, LANES))

    def second(i, acc):
        zz, zy, zm, by, zb = acc
        for j in range(STEPS):
            b, m, n = sb[at(i, j), :], sm[at(i, j), :], sn[at(i, j), :]
            z = m - mu_all * b
            q = n - mu_all * m
            zz, zy, zm = zz + z * z, zy + z * q, zm + z * m
            by, zb = by + b * q, zb + z * b
        return zz, zy, zm, by, zb

    rest = [whole(x) for x in lax.fori_loop(0, 32, second, (zero,) * 5)]
    lane_row = iota((1, LANES), 1)
    packed = jnp.zeros((1, LANES), jnp.float32)
    for j, x in enumerate([bb, bm, mu] + rest):
        packed = jnp.where(lane_row == j, x, packed)
    sums[...] = jnp.broadcast_to(packed, sums.shape)


def spread_kernel(where_ref, sb, sm, sn, keep, send, T, HI, MID, FLAT):
    core = where_ref[1]
    t_row, t_lane = iota((LANES, LANES), 0), iota((LANES, LANES), 1)
    group = by_twelve(t_row)
    col = (t_row - group * SEGS) * STEPS - LEFT
    for j in range(STEPS + 1):
        for t in range(GROUPS):
            hit = jnp.logical_and(group == t, col + j == t_lane) if j < STEPS else t_row < 0
            T[j * LANES : (j + 1) * LANES, t * LANES : (t + 1) * LANES] = as16(hit)
    for j in (STEPS,):
        HI[:, j * LANES : (j + 1) * LANES] = jnp.zeros((256, LANES), jnp.bfloat16)
        MID[:, j * LANES : (j + 1) * LANES] = jnp.zeros((256, LANES), jnp.bfloat16)
    for which, ref in enumerate((sb, sm, sn)):
        cube = ref.reshape(32, STEPS, 8, LANES)
        for j in range(STEPS):
            hi, mid = split_parts(cube[:, j].reshape(256, LANES), 2)
            HI[:, j * LANES : (j + 1) * LANES] = hi
            MID[:, j * LANES : (j + 1) * LANES] = mid
        for t in range(GROUPS // 2):
            lanes = slice(2 * t * LANES, 2 * (t + 1) * LANES)
            pair = dot(HI[...], T[:, lanes]) + dot(MID[...], T[:, lanes])
            FLAT[2 * t * 256 : (2 * t + 1) * 256, :] = pair[:, :LANES]
            FLAT[(2 * t + 1) * 256 : (2 * t + 2) * 256, :] = pair[:, LANES:]
        for target, rows in ((keep, core), (send, 1 - core)):
            for s in range(8):
                for t in range(GROUPS):
                    for jj in range(2):
                        target[which, GROUPS * s + t, 8 * jj : 8 * jj + 8, :] = FLAT[
                            pl.ds(t * 256 + (rows * BAND + 8 * jj) * 8 + s, 8, stride=8), :
                        ]


def last_kernel(where_ref, sums, keep, got, increment, residual):
    core = where_ref[1]
    table = sums[...]

    def col(j):
        return table[:, j : j + 1]

    def total(x):
        return jnp.sum(x, axis=0, keepdims=True)

    bb, bm, mus, zz, zy, zm, by, zb = (col(j) for j in range(8))
    rr = total(bb)
    h = total(bm)
    mu = h / rr
    off = mus - mu
    a1 = rr / (rr + h)
    z_z = total(zz + 2.0 * off * zb + off * off * bb)
    z_m = total(zm + off * bm)
    b_q = total(by + off * bm)
    z_q = total(zy + off * (zm + by) + off * off * bm)
    new = a1 * a1 * z_z
    beta = new / rr
    size = new + beta * beta * rr
    curve = size + a1 * a1 * z_q - a1 * beta * (z_m + b_q) + beta * beta * h
    a2 = new / curve
    spread = lambda x: jnp.broadcast_to(x, (8, LANES))
    mu, a1, a2, beta = spread(mu), spread(a1), spread(a2), spread(beta)

    def write(ref, idx, channel):
        for j in range(2):
            here = slice(8 * j, 8 * j + 8)
            b, m, n = ref[0, idx, here, :], ref[1, idx, here, :], ref[2, idx, here, :]
            r = a1 * (mu * b - m)
            image = a1 * (mu * m - n) + beta * m
            d = r + beta * b
            increment[channel, here, :] = a1 * b + a2 * d
            residual[channel, here, :] = r - a2 * (d + image)

    for ref, half in ((keep, core), (got, 1 - core)):

        def one(i, carry):
            write(ref, i, HALF * half + i)
            return carry

        lax.fori_loop(0, jnp.where(half == 0, HALF, increment.shape[0] - HALF), one, 0)


def spec(memory_space=pltpu.VMEM):
    return pl.BlockSpec(memory_space=memory_space)


def scratch():
    f32 = jnp.float32
    return [
        pltpu.VMEM(((ROWS + 1) * LINE, LANES), f32),
        pltpu.VMEM(((ROWS + 1) * LINE, LANES), f32),
        pltpu.VMEM((ROWS * LINE, LANES), f32),
        pltpu.VMEM((ROWS * LINE, LANES), f32),
        pltpu.VMEM((ROWS * LINE, LANES), f32),
        pltpu.VMEM((ROWS * STEPS, LANES), f32),
        pltpu.VMEM((5 * STEPS, ROWS, LANES), f32),
        pltpu.VMEM((3, 256, 9 * LANES), jnp.bfloat16),
    ]


def local(
    kappa_east, kappa_north, depth, sigma, obs_precision, obs_tile, obs_col, obs_lat, innovation
):
    f32 = jnp.float32
    channels = sigma.shape[0]
    lon_tiles = lax.axis_size("lon")
    lat_tiles = lax.axis_size("lat")
    lat_here = lax.axis_index("lat")
    place = jnp.stack([lat_here // 2, lat_here % 2]).astype(jnp.int32)
    core = lat_here % 2
    params = pltpu.CompilerParams(vmem_limit_bytes=VMEM_LIMIT)

    packed = pl.pallas_call(
        lambda *refs: pack_kernel(lon_tiles, *refs),
        out_shape=jax.ShapeDtypeStruct((lon_tiles, lat_tiles, CAP, 256), f32),
        in_specs=[spec()] * 5,
        out_specs=spec(),
        scratch_shapes=[pltpu.VMEM((2 * HALF, LANES), f32)],
        compiler_params=params,
        name="pack",
    )(
        obs_tile,
        obs_tile.reshape(1, LANES),
        obs_lat.reshape(1, LANES),
        obs_col.reshape(1, LANES),
        innovation,
    )
    recv = lax.all_to_all(
        packed.reshape(lon_tiles * lat_tiles, CAP, 256), ALL, 0, 0, tiled=True
    ).reshape(lon_tiles, lat_tiles, CAP, 256)

    stacked = jnp.stack([kappa_east, kappa_north, depth.astype(f32)])
    count = lon_tiles
    right = lax.ppermute(stacked[:, :, :EDGE], "lon", [((i + 1) % count, i) for i in range(count)])
    left = lax.ppermute(stacked[:, :, -EDGE:], "lon", [(i, (i + 1) % count) for i in range(count)])
    rim = jnp.concatenate([right, left, right, left], axis=2)
    geo = lax.all_gather(jnp.concatenate([stacked, rim]), "lat", axis=1, tiled=True)

    order = core * HALF + jnp.arange(HALF, dtype=jnp.int32)
    level = jnp.where(order < 2 * NZ, order % NZ, jnp.where(order < channels, 0, 1 << 20))
    pads = jnp.zeros((2 * HALF - channels,), f32)
    scale = lax.dynamic_slice_in_dim(jnp.concatenate([sigma, pads]), core * HALF, HALF)
    weight = lax.dynamic_slice_in_dim(jnp.concatenate([obs_precision, pads]), core * HALF, HALF)
    par = jnp.stack([level.astype(f32), scale * weight, scale * scale * weight])
    par = jnp.repeat(par.reshape(3, 8, GROUPS), SEGS, axis=2)
    fills = jnp.broadcast_to(jnp.array([1 << 20, 0, 0], f32)[:, None, None], (3, 8, 8))
    par = jnp.concatenate([par, fills], axis=2)

    series = jax.ShapeDtypeStruct((32 * LINE, LANES), f32)
    sb, sm, sn, sums = pl.pallas_call(
        main_kernel,
        out_shape=(
            series,
            series,
            series,
            jax.ShapeDtypeStruct((lon_tiles * lat_tiles, LANES), f32),
        ),
        in_specs=[spec(pltpu.SMEM), spec(), spec(), spec()],
        out_specs=(spec(), spec(), spec(), spec()),
        scratch_shapes=scratch(),
        compiler_params=params,
        name="iterate",
    )(place, recv, geo, par)

    sums = lax.all_to_all(sums, ALL, 0, 0, tiled=True)
    tile_shape = jax.ShapeDtypeStruct((3, HALF, BAND, LANES), f32)
    keep, send = pl.pallas_call(
        spread_kernel,
        out_shape=(tile_shape, tile_shape),
        in_specs=[spec(pltpu.SMEM), spec(), spec(), spec()],
        out_specs=(spec(), spec()),
        scratch_shapes=[
            pltpu.VMEM((16 * LANES, GROUPS * LANES), jnp.bfloat16),
            pltpu.VMEM((256, 16 * LANES), jnp.bfloat16),
            pltpu.VMEM((256, 16 * LANES), jnp.bfloat16),
            pltpu.VMEM((GROUPS * 256, LANES), f32),
        ],
        compiler_params=params,
        cost_estimate=pl.CostEstimate(flops=8_000_000_000, bytes_accessed=10_000_000, transcendentals=0),
        name="spread",
    )(place, sb, sm, sn)
    send, sums = lax.optimization_barrier((send, sums))
    got = lax.ppermute(send, "lat", [(i, i ^ 1) for i in range(lat_tiles)])
    out = jax.ShapeDtypeStruct((channels, BAND, LANES), f32)
    return pl.pallas_call(
        last_kernel,
        out_shape=(out, out),
        in_specs=[spec(pltpu.SMEM), spec(), spec(), spec()],
        out_specs=(spec(), spec()),
        compiler_params=params,
        name="combine",
    )(place, sums, keep, got)


def solution(mesh):
    return jax.shard_map(
        local,
        mesh=mesh,
        in_specs=(
            P("lat", "lon"),
            P("lat", "lon"),
            P("lat", "lon"),
            P(),
            P(),
            P(("lon", "lat"), None),
            P(("lon", "lat")),
            P(("lon", "lat")),
            P(None, ("lon", "lat")),
        ),
        out_specs=(P(None, "lat", "lon"), P(None, "lat", "lon")),
        check_vma=False,
    )
```

```python
import jax
import jax.numpy as jnp
from jax import lax
from jax.experimental import pallas as pl
from jax.experimental.pallas import tpu as pltpu
from jax.sharding import PartitionSpec as P

NZ = 75
CAP = 8
HALF = 80
GROUPS = 10
SEGS = 12
STEPS = 15
LEFT = 26
ROWS = 64
NEED = 57
LANES = 128
EDGE = 32
BAND = 16
CHUNK = 8
LINE = STEPS * 8
ALL = ("lon", "lat")
MIB = 1024 * 1024
VMEM_LIMIT = 60 * MIB


def split_parts(x, count):
    parts = []
    for step in range(count):
        part = x.astype(jnp.bfloat16)
        parts.append(part)
        if step + 1 < count:
            x = x - part.astype(jnp.float32)
    return parts


def iota(shape, axis):
    return lax.broadcasted_iota(jnp.int32, shape, axis)


def by_twelve(x):
    return lax.shift_right_logical(x * 5462, 16)


def by_fifteen(x):
    return lax.shift_right_logical(x * 4370, 16)


def as16(mask):
    return jnp.where(mask, 1.0, 0.0).astype(jnp.bfloat16)


def dot(a, b):
    return jnp.dot(a, b, preferred_element_type=jnp.float32)


def dot_nt(a, b):
    return lax.dot_general(a, b, (((1,), (1,)), ((), ())), preferred_element_type=jnp.float32)


def pack_kernel(tiles, tile_row, obs_lat, obs_col, values, out, wide):
    channels = values.shape[0]
    wide[144:160, :] = jnp.zeros((16, LANES), jnp.float32)
    wide[0:channels, :] = values[...]
    trow = tile_row[...]
    every = jnp.broadcast_to(trow, (LANES, LANES))
    seen = jnp.logical_and(
        every.T == every, iota((LANES, LANES), 0) < iota((LANES, LANES), 1)
    )
    rank = jnp.sum(jnp.where(seen, 1.0, 0.0), axis=0, keepdims=True).astype(jnp.int32)
    slots = iota((tiles * CAP, LANES), 0)
    lines = iota((16, LANES), 0)
    marks, codes = [], []
    for block, (shift, base) in enumerate(((0, LEFT), (1, LEFT - LANES), (tiles - 1, LEFT + LANES))):
        at = lax.rem(trow + shift, tiles) * CAP + rank
        marks.append(as16(slots == at))
        u = obs_col[...] + base
        seg = by_fifteen(jnp.maximum(u, 0))
        good = jnp.logical_and(u >= 0, u < SEGS * STEPS)
        code = jnp.where(good, obs_lat[...] * STEPS + u - seg * STEPS + 1, 0)
        codes.append(
            jnp.where(
                lines == 2 * block,
                code.astype(jnp.float32),
                jnp.where(lines == 2 * block + 1, seg.astype(jnp.float32), 0.0),
            )
        )
    blank = jnp.zeros((HALF, LANES), jnp.float32)
    for half in range(2):
        vals = wide[half * HALF : (half + 1) * HALF, :]
        total = None
        for block in range(3):
            pieces = [vals if j == block else blank for j in range(3)] + [codes[block]]
            for part in split_parts(jnp.concatenate(pieces, axis=0), 3):
                term = dot_nt(marks[block], part)
                total = term if total is None else total + term
        cube = total.reshape(tiles, CAP, 256)
        out[:, half] = cube
        out[:, 2 + half] = cube


def main_kernel(
    where_ref, recv, geo, par, out_b, out_m, out_n, sums, V, W, FE, FN, DC, CNT, G, EXP, sb, sm, sn, done
):
    y = where_ref[0]
    lane = iota((8, LANES), 1)
    seg8 = jnp.where(lane < GROUPS * SEGS, lane - by_twelve(lane) * SEGS, -1)

    own = [geo[f] for f in range(3)]
    both = [jnp.concatenate([geo[f], geo[3 + f]], axis=1) for f in range(3)]
    wide_lane, wide_row = iota((ROWS, 256), 1), iota((ROWS, 256), 0)
    ke, kn, d = both
    kn = jnp.where(wide_row == ROWS - 1, 0.0, kn)
    east = jnp.where(
        wide_lane == LANES + 2 * EDGE - 1,
        jnp.concatenate([pltpu.roll(own[2], 63, 1)] * 2, axis=1),
        pltpu.roll(d, 255, 1),
    )
    fields = (ke, jnp.minimum(d, east), kn, jnp.minimum(d, pltpu.roll(d, ROWS - 1, 0)), d)
    q_lane, q_row = iota((256, LANES), 1), iota((256, LANES), 0)
    q_col = (q_lane - by_twelve(q_lane) * SEGS) * STEPS - LEFT
    parts = [split_parts(x, 3 if f in (0, 2) else 1) for f, x in enumerate(fields)]
    for j in range(STEPS):
        col = q_col + j
        perm = as16(q_row == jnp.where(col < 0, LANES + 2 * EDGE + col, col))
        for f in range(5):
            total = None
            for part in parts[f]:
                term = dot(part, perm)
                total = term if total is None else total + term
            G[f * STEPS + j] = total

    e_lane = iota((256, LANES), 1)
    e_group, e_row = by_twelve(e_lane), iota((256, LANES), 0)
    for g in range(3):
        for s in range(8):
            hit = jnp.logical_and(e_group < GROUPS, e_row == HALF * g + GROUPS * s + e_group)
            EXP[g, :, s * LANES : (s + 1) * LANES] = as16(hit)
        EXP[g, :, 8 * LANES : 9 * LANES] = as16(e_row == 3 * HALF + 2 * g + 1)

    pick = as16(iota((16, 256), 1) == 3 * HALF + iota((16, 256), 0))
    seg_of = jnp.where(e_lane < GROUPS * SEGS, e_lane - e_group * SEGS, -1).astype(jnp.float32)
    cell = (iota((BAND * STEPS, 256), 0) + 1).astype(jnp.float32)

    def band(k, carry):
        hi, mid = split_parts(recv[:, k].reshape(256, 256), 2)
        codes = dot_nt(pick, hi)
        acc, count = None, None
        for g in range(3):
            left = as16(cell == codes[2 * g : 2 * g + 1])
            full = dot(hi, EXP[g])
            rest = dot(mid, EXP[g, :, 0 : 8 * LANES])
            hot = seg_of == full[:, 8 * LANES :]
            for source in (full, rest):
                right = jnp.concatenate(
                    [
                        jnp.where(hot, source[:, s * LANES : (s + 1) * LANES], 0.0).astype(jnp.bfloat16)
                        for s in range(8)
                    ],
                    axis=1,
                )
                term = dot(left, right)
                acc = term if acc is None else acc + term
            term = dot(left, as16(hot))
            count = term if count is None else count + term
        base = k * (BAND * STEPS)
        for s in range(8):
            V[pl.ds(base * 8 + s, BAND * STEPS, stride=8), :] = acc[:, s * LANES : (s + 1) * LANES]
        CNT[pl.ds(pl.multiple_of(base, 8), BAND * STEPS), :] = count
        return carry

    lax.fori_loop(0, recv.shape[1], band, 0)

    def at(row, j):
        return pl.ds(pl.multiple_of(row * LINE + 8 * j, 8), 8)

    level, w_all, s_all = par[0], par[1], par[2]

    def fill(row, carry):
        for j in range(STEPS):
            ke, de, kn, dn, d = [
                G[f * STEPS + j, pl.ds(row, 1), :] for f in range(5)
            ]
            here = at(row, j)
            FE[here, :] = jnp.where(de > level, ke, 0.0)
            FN[here, :] = jnp.where(dn > level, kn, 0.0)
            wet = d > level
            V[here, :] = jnp.where(wet, V[here, :] * w_all, 0.0)
            DC[here, :] = jnp.where(wet, CNT[pl.ds(row * STEPS + j, 1), :] * s_all, 0.0)
        return carry

    lax.fori_loop(0, ROWS, fill, 0)
    for ref in (V, W):
        ref[ROWS * LINE : (ROWS + 1) * LINE, :] = jnp.zeros((LINE, LANES), jnp.float32)

    def sweep(src, dst, number, weighted=False):
        chunks = lax.div(NEED - number + CHUNK - 1, CHUNK)
        start = y * (ROWS - CHUNK * chunks)

        def one(c, carry):
            v, gone = list(carry[:STEPS]), list(carry[STEPS:])
            base = start + c * CHUNK
            for i in range(CHUNK):
                north = [src[at(base + i + 1, j), :] for j in range(STEPS)]
                flux = [None] * STEPS
                last = STEPS - 1
                flux[last] = FE[at(base + i, last), :] * (pltpu.roll(v[0], LANES - 1, 1) - v[last])
                west = pltpu.roll(flux[last], 1, 1)
                for j in range(last):
                    flux[j] = FE[at(base + i, j), :] * (v[j + 1] - v[j])
                for j in list(range(1, STEPS)) + [0]:
                    rise = FN[at(base + i, j), :] * (north[j] - v[j])
                    out = (v[j] + flux[j]) - (flux[j - 1] if j else west) + (rise - gone[j])
                    if weighted:
                        out = out * DC[at(base + i, j), :]
                    dst[at(base + i, j), :] = out
                    gone[j] = rise
                v = north
            return tuple(v) + tuple(gone)

        zero = jnp.zeros((8, LANES), jnp.float32)
        below = jnp.maximum(start - 1, 0)
        v = tuple(src[at(start, j), :] for j in range(STEPS))
        gone = tuple(
            jnp.where(y > 0, FN[at(below, j), :] * (v[j] - src[at(below, j), :]), zero)
            for j in range(STEPS)
        )
        lax.fori_loop(0, chunks, one, v + gone)

    def smooth(src, dst, stage, weighted=False):
        def twice(step, carry):
            number = 5 * stage + 1 + 2 * step
            sweep(src, dst, number)
            sweep(dst, src, number + 1)
            return carry

        lax.fori_loop(0, 2, twice, 0)
        sweep(src, dst, 5 * stage + 5, weighted)

    zero = jnp.zeros((8, LANES), jnp.float32)

    def mine(j):
        u = seg8 * STEPS + j
        return jnp.logical_and(u >= LEFT, u < LEFT + LANES)

    def whole(x):
        return jnp.sum(jnp.sum(x, axis=0, keepdims=True), axis=1, keepdims=True)

    def save(src, ref, use, count):
        def one(i, carry):
            acc = list(carry)
            for j in range(STEPS):
                x = jnp.where(mine(j), src[at(y * 32 + i, j), :], 0.0)
                ref[at(i, j), :] = x
                if count:
                    for n, term in enumerate(use(x, at(i, j))):
                        acc[n * 3 + j % 3] = acc[n * 3 + j % 3] + term
            return tuple(acc)

        acc = lax.fori_loop(0, 32, one, (zero,) * (3 * count))
        return [whole(acc[3 * n] + acc[3 * n + 1] + acc[3 * n + 2]) for n in range(count)]

    smooth(V, W, 0)
    save(W, sb, None, 0)
    copies = [
        pltpu.make_async_copy(ref, out, done.at[n])
        for n, (ref, out) in enumerate(((sb, out_b), (sm, out_m), (sn, out_n)))
    ]
    copies[0].start()
    smooth(W, V, 1, True)
    smooth(V, W, 2)

    def first(m, here):
        b = sb[here, :]
        return b * b, b * m

    bb, bm = save(W, sm, first, 2)
    copies[1].start()
    mu = jnp.where(bb > 0.0, bm / jnp.where(bb > 0.0, bb, 1.0), 0.0)
    smooth(W, V, 3, True)
    smooth(V, W, 4)
    mu_all = jnp.broadcast_to(mu, (8, LANES))

    def second(n, here):
        b, m = sb[here, :], sm[here, :]
        z = m - mu_all * b
        q = n - mu_all * m
        return z * z, z * q, z * m, b * q, z * b

    rest = save(W, sn, second, 5)
    copies[2].start()
    lane_row = iota((1, LANES), 1)
    packed = jnp.zeros((1, LANES), jnp.float32)
    for j, x in enumerate([bb, bm, mu] + rest):
        packed = jnp.where(lane_row == j, x, packed)
    sums[...] = jnp.broadcast_to(packed, sums.shape)
    for copy in copies:
        copy.wait()


def spread_kernel(where_ref, sb, sm, sn, keep, send, T, HI, MID, FLAT, HELD, ready):
    core = where_ref[1]
    copies = [
        pltpu.make_async_copy(ref, HELD.at[n], ready.at[n]) for n, ref in enumerate((sb, sm, sn))
    ]
    for copy in copies:
        copy.start()
    t_row, t_lane = iota((LANES, LANES), 0), iota((LANES, LANES), 1)
    group = by_twelve(t_row)
    col = (t_row - group * SEGS) * STEPS - LEFT
    for t in range(GROUPS):
        goal = jnp.where(group == t, col, -LANES * STEPS) - t_lane
        for j in range(STEPS):
            T[j * LANES : (j + 1) * LANES, t * LANES : (t + 1) * LANES] = as16(goal == -j)
    for which in range(3):
        copies[which].wait()
        cube = HELD.reshape(3, 32, STEPS, 8, LANES)
        for j in range(STEPS):
            hi, mid = split_parts(cube[which, :, j].reshape(256, LANES), 2)
            HI[:, j * LANES : (j + 1) * LANES] = hi
            MID[:, j * LANES : (j + 1) * LANES] = mid
        for t in range(GROUPS // 2):
            lanes = slice(2 * t * LANES, 2 * (t + 1) * LANES)
            pair = dot(HI[...], T[:, lanes]) + dot(MID[...], T[:, lanes])
            for n in range(2):
                FLAT[2 * t + n] = pair[:, n * LANES : (n + 1) * LANES]
        for target, rows in ((keep, core), (send, 1 - core)):
            for s in range(8):
                for t in range(GROUPS):
                    for jj in range(2):
                        target[which, GROUPS * s + t, 8 * jj : 8 * jj + 8, :] = FLAT[
                            t, pl.ds((rows * BAND + 8 * jj) * 8 + s, 8, stride=8), :
                        ]


def last_kernel(where_ref, sums, keep, got, increment, residual, held):
    half = pl.program_id(0) // 2

    def scalars():
        table = sums[...].T

        def total(x):
            return jnp.sum(x, axis=1, keepdims=True)

        bb, bm, mus, zz, zy, zm, by, zb = (table[j : j + 1] for j in range(8))
        rr = total(bb)
        h = total(bm)
        mu = h / rr
        off = mus - mu
        a1 = rr / (rr + h)
        z_z = total(zz + 2.0 * off * zb + off * off * bb)
        z_m = total(zm + off * bm)
        b_q = total(by + off * bm)
        z_q = total(zy + off * (zm + by) + off * off * bm)
        new = a1 * a1 * z_z
        beta = new / rr
        size = new + beta * beta * rr
        curve = size + a1 * a1 * z_q - a1 * beta * (z_m + b_q) + beta * beta * h
        for n, x in enumerate((mu, a1, new / curve, beta)):
            held[n] = jnp.broadcast_to(x, (8, LANES))

    pl.when(pl.program_id(0) == 0)(scalars)
    mu, a1, a2, beta = (held[n] for n in range(4))

    def write(ref):
        def one(i, carry):
            for c in range(8):
                for j in range(2):
                    at = (i * 8 + c, slice(8 * j, 8 * j + 8))
                    b, m, n = ref[(0,) + at], ref[(1,) + at], ref[(2,) + at]
                    r = a1 * (mu * b - m)
                    image = a1 * (mu * m - n) + beta * m
                    d = r + beta * b
                    increment[at] = a1 * b + a2 * d
                    residual[at] = r - a2 * (d + image)
            return carry

        lax.fori_loop(0, HALF // 16, one, 0)

    pl.when(half == where_ref[1])(lambda: write(keep))
    pl.when(half != where_ref[1])(lambda: write(got))


def spec(memory_space=pltpu.VMEM):
    return pl.BlockSpec(memory_space=memory_space)


def scratch():
    f32 = jnp.float32
    return [
        pltpu.VMEM(((ROWS + 1) * LINE, LANES), f32),
        pltpu.VMEM(((ROWS + 1) * LINE, LANES), f32),
        pltpu.VMEM((ROWS * LINE, LANES), f32),
        pltpu.VMEM((ROWS * LINE, LANES), f32),
        pltpu.VMEM((ROWS * LINE, LANES), f32),
        pltpu.VMEM((ROWS * STEPS, LANES), f32),
        pltpu.VMEM((5 * STEPS, ROWS, LANES), f32),
        pltpu.VMEM((3, 256, 9 * LANES), jnp.bfloat16),
        pltpu.VMEM((32 * LINE, LANES), f32),
        pltpu.VMEM((32 * LINE, LANES), f32),
        pltpu.VMEM((32 * LINE, LANES), f32),
        pltpu.SemaphoreType.DMA((3,)),
    ]


def local(
    kappa_east, kappa_north, depth, sigma, obs_precision, obs_tile, obs_col, obs_lat, innovation
):
    f32 = jnp.float32
    channels = sigma.shape[0]
    lon_tiles = lax.axis_size("lon")
    lat_tiles = lax.axis_size("lat")
    lat_here = lax.axis_index("lat")
    place = jnp.stack([lat_here // 2, lat_here % 2]).astype(jnp.int32)
    core = lat_here % 2
    params = lambda size: pltpu.CompilerParams(vmem_limit_bytes=size)

    packed = pl.pallas_call(
        lambda *refs: pack_kernel(lon_tiles, *refs),
        out_shape=jax.ShapeDtypeStruct((lon_tiles, lat_tiles, CAP, 256), f32),
        in_specs=[spec()] * 4,
        out_specs=spec(),
        scratch_shapes=[pltpu.VMEM((2 * HALF, LANES), f32)],
        compiler_params=params(10 * MIB),
        name="pack",
    )(
        obs_tile.reshape(1, LANES),
        obs_lat.reshape(1, LANES),
        obs_col.reshape(1, LANES),
        innovation,
    )
    stacked = jnp.stack([kappa_east, kappa_north, depth.astype(f32)])
    count = lon_tiles
    right = lax.ppermute(stacked[:, :, :EDGE], "lon", [((i + 1) % count, i) for i in range(count)])
    left = lax.ppermute(stacked[:, :, -EDGE:], "lon", [(i, (i + 1) % count) for i in range(count)])
    recv = lax.all_to_all(
        packed.reshape(lon_tiles * lat_tiles, CAP, 256), ALL, 0, 0, tiled=True
    ).reshape(lon_tiles, lat_tiles, CAP, 256)

    rim = jnp.concatenate([right, left, right, left], axis=2)
    geo = lax.all_gather(jnp.concatenate([stacked, rim]), "lat", axis=1, tiled=True)

    order = core * HALF + jnp.arange(HALF, dtype=jnp.int32)
    level = jnp.where(order < 2 * NZ, order % NZ, jnp.where(order < channels, 0, 1 << 20))
    pads = jnp.zeros((2 * HALF - channels,), f32)
    scale = lax.dynamic_slice_in_dim(jnp.concatenate([sigma, pads]), core * HALF, HALF)
    weight = lax.dynamic_slice_in_dim(jnp.concatenate([obs_precision, pads]), core * HALF, HALF)
    par = jnp.stack([level.astype(f32), scale * weight, scale * scale * weight])
    par = jnp.repeat(par.reshape(3, 8, GROUPS), SEGS, axis=2)
    fills = jnp.broadcast_to(jnp.array([1 << 20, 0, 0], f32)[:, None, None], (3, 8, 8))
    par = jnp.concatenate([par, fills], axis=2)

    series = jax.ShapeDtypeStruct((32 * LINE, LANES), f32)
    sb, sm, sn, sums = pl.pallas_call(
        main_kernel,
        out_shape=(
            series,
            series,
            series,
            jax.ShapeDtypeStruct((lon_tiles * lat_tiles, LANES), f32),
        ),
        in_specs=[spec(pltpu.SMEM), spec(), spec(), spec()],
        out_specs=(spec(pltpu.HBM), spec(pltpu.HBM), spec(pltpu.HBM), spec()),
        scratch_shapes=scratch(),
        compiler_params=params(VMEM_LIMIT),
        name="iterate",
    )(place, recv, geo, par)

    sums = lax.all_to_all(sums, ALL, 0, 0, tiled=True)
    tile_shape = jax.ShapeDtypeStruct((3, HALF, BAND, LANES), f32)
    keep, send = pl.pallas_call(
        spread_kernel,
        out_shape=(tile_shape, tile_shape),
        in_specs=[spec(pltpu.SMEM)] + [spec(pltpu.HBM)] * 3,
        out_specs=(spec(), spec()),
        scratch_shapes=[
            pltpu.VMEM((STEPS * LANES, GROUPS * LANES), jnp.bfloat16),
            pltpu.VMEM((256, STEPS * LANES), jnp.bfloat16),
            pltpu.VMEM((256, STEPS * LANES), jnp.bfloat16),
            pltpu.VMEM((GROUPS, 256, LANES), f32),
            pltpu.VMEM((3, 32 * LINE, LANES), f32),
            pltpu.SemaphoreType.DMA((3,)),
        ],
        compiler_params=params(VMEM_LIMIT),
        cost_estimate=pl.CostEstimate(flops=8_000_000_000, bytes_accessed=10_000_000, transcendentals=0),
        name="spread",
    )(place, sb, sm, sn)
    send, sums = lax.optimization_barrier((send, sums))
    got = lax.ppermute(send, "lat", [(i, i ^ 1) for i in range(lat_tiles)])
    out = jax.ShapeDtypeStruct((channels, BAND, LANES), f32)
    early = lambda i: jnp.minimum(i, 1)
    late = lambda i: jnp.maximum(i - 2, 0)
    block = (3, HALF // 2, BAND, LANES)
    return pl.pallas_call(
        last_kernel,
        out_shape=(out, out),
        grid_spec=pltpu.PrefetchScalarGridSpec(
            num_scalar_prefetch=1,
            grid=(4,),
            in_specs=[
                pl.BlockSpec((lon_tiles * lat_tiles, LANES), lambda i, w: (0, 0)),
                pl.BlockSpec(block, lambda i, w: (0, jnp.where(w[1] == 0, early(i), late(i)), 0, 0)),
                pl.BlockSpec(block, lambda i, w: (0, jnp.where(w[1] == 0, late(i), early(i)), 0, 0)),
            ],
            out_specs=(
                pl.BlockSpec((HALF // 2, BAND, LANES), lambda i, w: (i, 0, 0)),
                pl.BlockSpec((HALF // 2, BAND, LANES), lambda i, w: (i, 0, 0)),
            ),
            scratch_shapes=[pltpu.VMEM((4, 8, LANES), f32)],
        ),
        compiler_params=params(16 * MIB),
        name="combine",
    )(place, sums, keep, got)


def solution(mesh):
    return jax.shard_map(
        local,
        mesh=mesh,
        in_specs=(
            P("lat", "lon"),
            P("lat", "lon"),
            P("lat", "lon"),
            P(),
            P(),
            P(("lon", "lat"), None),
            P(("lon", "lat")),
            P(("lon", "lat")),
            P(None, ("lon", "lat")),
        ),
        out_specs=(P(None, "lat", "lon"), P(None, "lat", "lon")),
        check_vma=False,
    )
```

```python
import jax
import jax.numpy as jnp
from jax import lax
from jax.experimental import pallas as pl
from jax.experimental.pallas import tpu as pltpu
from jax.sharding import PartitionSpec as P

NZ = 75
CAP = 8
HALF = 80
GROUPS = 10
SEGS = 12
STEPS = 15
LEFT = 26
ROWS = 64
NEED = 57
LANES = 128
EDGE = 32
BAND = 16
CHUNK = 8
LINE = STEPS * 8
ALL = ("lon", "lat")
MIB = 1024 * 1024
VMEM_LIMIT = 60 * MIB


def split_parts(x, count):
    parts = []
    for step in range(count):
        part = x.astype(jnp.bfloat16)
        parts.append(part)
        if step + 1 < count:
            x = x - part.astype(jnp.float32)
    return parts


def iota(shape, axis):
    return lax.broadcasted_iota(jnp.int32, shape, axis)


def by_twelve(x):
    return lax.shift_right_logical(x * 5462, 16)


def by_fifteen(x):
    return lax.shift_right_logical(x * 4370, 16)


def as16(mask):
    return jnp.where(mask, 1.0, 0.0).astype(jnp.bfloat16)


def dot(a, b):
    return jnp.dot(a, b, preferred_element_type=jnp.float32)


def dot_nt(a, b):
    return lax.dot_general(a, b, (((1,), (1,)), ((), ())), preferred_element_type=jnp.float32)


def pack_kernel(tiles, tile_row, obs_lat, obs_col, values, out, wide):
    channels = values.shape[0]
    wide[144:160, :] = jnp.zeros((16, LANES), jnp.float32)
    wide[0:channels, :] = values[...]
    trow = tile_row[...]
    every = jnp.broadcast_to(trow, (LANES, LANES))
    seen = jnp.logical_and(
        every.T == every, iota((LANES, LANES), 0) < iota((LANES, LANES), 1)
    )
    rank = jnp.sum(jnp.where(seen, 1.0, 0.0), axis=0, keepdims=True).astype(jnp.int32)
    slots = iota((tiles * CAP, LANES), 0)
    lines = iota((16, LANES), 0)
    marks, codes = [], []
    for block, (shift, base) in enumerate(((0, LEFT), (1, LEFT - LANES), (tiles - 1, LEFT + LANES))):
        at = lax.rem(trow + shift, tiles) * CAP + rank
        marks.append(as16(slots == at))
        u = obs_col[...] + base
        seg = by_fifteen(jnp.maximum(u, 0))
        good = jnp.logical_and(u >= 0, u < SEGS * STEPS)
        code = jnp.where(good, obs_lat[...] * STEPS + u - seg * STEPS + 1, 0)
        codes.append(
            jnp.where(
                lines == 2 * block,
                code.astype(jnp.float32),
                jnp.where(lines == 2 * block + 1, seg.astype(jnp.float32), 0.0),
            )
        )
    blank = jnp.zeros((HALF, LANES), jnp.float32)
    for half in range(2):
        vals = wide[half * HALF : (half + 1) * HALF, :]
        total = None
        for block in range(3):
            pieces = [vals if j == block else blank for j in range(3)] + [codes[block]]
            for part in split_parts(jnp.concatenate(pieces, axis=0), 3):
                term = dot_nt(marks[block], part)
                total = term if total is None else total + term
        cube = total.reshape(tiles, CAP, 256)
        out[:, half] = cube
        out[:, 2 + half] = cube


def main_kernel(
    where_ref, recv, geo, par, out_b, out_m, out_n, sums, V, W, FE, FN, DC, CNT, G, EXP, sb, sm, sn, done
):
    y = where_ref[0]
    lane = iota((8, LANES), 1)
    seg8 = jnp.where(lane < GROUPS * SEGS, lane - by_twelve(lane) * SEGS, -1)

    own = [geo[f] for f in range(3)]
    both = [jnp.concatenate([geo[f], geo[3 + f]], axis=1) for f in range(3)]
    wide_lane, wide_row = iota((ROWS, 256), 1), iota((ROWS, 256), 0)
    ke, kn, d = both
    kn = jnp.where(wide_row == ROWS - 1, 0.0, kn)
    east = jnp.where(
        wide_lane == LANES + 2 * EDGE - 1,
        jnp.concatenate([pltpu.roll(own[2], 63, 1)] * 2, axis=1),
        pltpu.roll(d, 255, 1),
    )
    fields = (ke, jnp.minimum(d, east), kn, jnp.minimum(d, pltpu.roll(d, ROWS - 1, 0)), d)
    q_lane, q_row = iota((256, LANES), 1), iota((256, LANES), 0)
    q_col = (q_lane - by_twelve(q_lane) * SEGS) * STEPS - LEFT
    parts = [split_parts(x, 3 if f in (0, 2) else 1) for f, x in enumerate(fields)]
    for j in range(STEPS):
        col = q_col + j
        perm = as16(q_row == jnp.where(col < 0, LANES + 2 * EDGE + col, col))
        for f in range(5):
            total = None
            for part in parts[f]:
                term = dot(part, perm)
                total = term if total is None else total + term
            G[f * STEPS + j] = total

    e_lane = iota((256, LANES), 1)
    e_group, e_row = by_twelve(e_lane), iota((256, LANES), 0)
    for g in range(3):
        for s in range(8):
            hit = jnp.logical_and(e_group < GROUPS, e_row == HALF * g + GROUPS * s + e_group)
            EXP[g, :, s * LANES : (s + 1) * LANES] = as16(hit)
        EXP[g, :, 8 * LANES : 9 * LANES] = as16(e_row == 3 * HALF + 2 * g + 1)

    pick = as16(iota((16, 256), 1) == 3 * HALF + iota((16, 256), 0))
    seg_of = jnp.where(e_lane < GROUPS * SEGS, e_lane - e_group * SEGS, -1).astype(jnp.float32)
    cell = (iota((BAND * STEPS, 256), 0) + 1).astype(jnp.float32)

    def band(k, carry):
        hi, mid = split_parts(recv[:, k].reshape(256, 256), 2)
        codes = dot_nt(pick, hi)
        acc, count = None, None
        for g in range(3):
            left = as16(cell == codes[2 * g : 2 * g + 1])
            full = dot(hi, EXP[g])
            rest = dot(mid, EXP[g, :, 0 : 8 * LANES])
            hot = seg_of == full[:, 8 * LANES :]
            for source in (full, rest):
                right = jnp.concatenate(
                    [
                        jnp.where(hot, source[:, s * LANES : (s + 1) * LANES], 0.0).astype(jnp.bfloat16)
                        for s in range(8)
                    ],
                    axis=1,
                )
                term = dot(left, right)
                acc = term if acc is None else acc + term
            term = dot(left, as16(hot))
            count = term if count is None else count + term
        base = k * (BAND * STEPS)
        for s in range(8):
            V[pl.ds(base * 8 + s, BAND * STEPS, stride=8), :] = acc[:, s * LANES : (s + 1) * LANES]
        CNT[pl.ds(pl.multiple_of(base, 8), BAND * STEPS), :] = count
        return carry

    lax.fori_loop(0, recv.shape[1], band, 0)

    def at(row, j):
        return pl.ds(pl.multiple_of(row * LINE + 8 * j, 8), 8)

    level, w_all, s_all = par[0], par[1], par[2]

    def fill(row, carry):
        for j in range(STEPS):
            ke, de, kn, dn, d = [
                G[f * STEPS + j, pl.ds(row, 1), :] for f in range(5)
            ]
            here = at(row, j)
            FE[here, :] = jnp.where(de > level, ke, 0.0)
            FN[here, :] = jnp.where(dn > level, kn, 0.0)
            wet = d > level
            V[here, :] = jnp.where(wet, V[here, :] * w_all, 0.0)
            DC[here, :] = jnp.where(wet, CNT[pl.ds(row * STEPS + j, 1), :] * s_all, 0.0)
        return carry

    lax.fori_loop(0, ROWS, fill, 0)
    for ref in (V, W):
        ref[ROWS * LINE : (ROWS + 1) * LINE, :] = jnp.zeros((LINE, LANES), jnp.float32)

    def sweep(src, dst, number, weighted=False):
        chunks = lax.div(NEED - number + CHUNK - 1, CHUNK)
        start = y * (ROWS - CHUNK * chunks)

        def one(c, carry):
            v, gone = list(carry[:STEPS]), list(carry[STEPS:])
            base = start + c * CHUNK
            for i in range(CHUNK):
                north = [src[at(base + i + 1, j), :] for j in range(STEPS)]
                flux = [None] * STEPS
                last = STEPS - 1
                flux[last] = FE[at(base + i, last), :] * (pltpu.roll(v[0], LANES - 1, 1) - v[last])
                west = pltpu.roll(flux[last], 1, 1)
                for j in range(last):
                    flux[j] = FE[at(base + i, j), :] * (v[j + 1] - v[j])
                for j in list(range(1, STEPS)) + [0]:
                    rise = FN[at(base + i, j), :] * (north[j] - v[j])
                    out = (v[j] + flux[j]) - (flux[j - 1] if j else west) + (rise - gone[j])
                    if weighted:
                        out = out * DC[at(base + i, j), :]
                    dst[at(base + i, j), :] = out
                    gone[j] = rise
                v = north
            return tuple(v) + tuple(gone)

        zero = jnp.zeros((8, LANES), jnp.float32)
        below = jnp.maximum(start - 1, 0)
        v = tuple(src[at(start, j), :] for j in range(STEPS))
        gone = tuple(
            jnp.where(y > 0, FN[at(below, j), :] * (v[j] - src[at(below, j), :]), zero)
            for j in range(STEPS)
        )
        lax.fori_loop(0, chunks, one, v + gone)

    def smooth(src, dst, stage, weighted=False):
        def twice(step, carry):
            number = 5 * stage + 1 + 2 * step
            sweep(src, dst, number)
            sweep(dst, src, number + 1)
            return carry

        lax.fori_loop(0, 2, twice, 0)
        sweep(src, dst, 5 * stage + 5, weighted)

    zero = jnp.zeros((8, LANES), jnp.float32)

    def mine(j):
        u = seg8 * STEPS + j
        return jnp.logical_and(u >= LEFT, u < LEFT + LANES)

    def whole(x):
        return jnp.sum(jnp.sum(x, axis=0, keepdims=True), axis=1, keepdims=True)

    def save(src, ref, use, count):
        def one(i, carry):
            acc = list(carry)
            for j in range(STEPS):
                x = jnp.where(mine(j), src[at(y * 32 + i, j), :], 0.0)
                ref[at(i, j), :] = x
                if count:
                    for n, term in enumerate(use(x, at(i, j))):
                        acc[n * 3 + j % 3] = acc[n * 3 + j % 3] + term
            return tuple(acc)

        acc = lax.fori_loop(0, 32, one, (zero,) * (3 * count))
        return [whole(acc[3 * n] + acc[3 * n + 1] + acc[3 * n + 2]) for n in range(count)]

    smooth(V, W, 0)
    save(W, sb, None, 0)
    copies = [
        pltpu.make_async_copy(ref, out, done.at[n])
        for n, (ref, out) in enumerate(((sb, out_b), (sm, out_m), (sn, out_n)))
    ]
    copies[0].start()
    smooth(W, V, 1, True)
    smooth(V, W, 2)

    def first(m, here):
        b = sb[here, :]
        return b * b, b * m

    bb, bm = save(W, sm, first, 2)
    copies[1].start()
    mu = jnp.where(bb > 0.0, bm / jnp.where(bb > 0.0, bb, 1.0), 0.0)
    smooth(W, V, 3, True)
    smooth(V, W, 4)
    mu_all = jnp.broadcast_to(mu, (8, LANES))

    def second(n, here):
        b, m = sb[here, :], sm[here, :]
        z = m - mu_all * b
        q = n - mu_all * m
        return z * z, z * q, z * m, b * q, z * b

    rest = save(W, sn, second, 5)
    copies[2].start()
    lane_row = iota((1, LANES), 1)
    packed = jnp.zeros((1, LANES), jnp.float32)
    for j, x in enumerate([bb, bm, mu] + rest):
        packed = jnp.where(lane_row == j, x, packed)
    sums[...] = jnp.broadcast_to(packed, sums.shape)
    for copy in copies:
        copy.wait()


def spread_kernel(where_ref, sb, sm, sn, keep, send, T, HI, MID, FLAT, HELD, ready):
    core = where_ref[1]
    copies = [
        pltpu.make_async_copy(ref, HELD.at[n], ready.at[n]) for n, ref in enumerate((sb, sm, sn))
    ]
    for copy in copies:
        copy.start()
    t_row, t_lane = iota((LANES, LANES), 0), iota((LANES, LANES), 1)
    group = by_twelve(t_row)
    col = (t_row - group * SEGS) * STEPS - LEFT
    for t in range(GROUPS):
        goal = jnp.where(group == t, col, -LANES * STEPS) - t_lane
        for j in range(STEPS):
            T[j * LANES : (j + 1) * LANES, t * LANES : (t + 1) * LANES] = as16(goal == -j)
    for which in range(3):
        copies[which].wait()
        cube = HELD.reshape(3, 32, STEPS, 8, LANES)
        for j in range(STEPS):
            hi, mid = split_parts(cube[which, :, j].reshape(256, LANES), 2)
            HI[:, j * LANES : (j + 1) * LANES] = hi
            MID[:, j * LANES : (j + 1) * LANES] = mid
        for t in range(GROUPS // 2):
            lanes = slice(2 * t * LANES, 2 * (t + 1) * LANES)
            pair = dot(HI[...], T[:, lanes]) + dot(MID[...], T[:, lanes])
            for n in range(2):
                FLAT[2 * t + n] = pair[:, n * LANES : (n + 1) * LANES]
        for target, rows in ((keep, core), (send, 1 - core)):
            for s in range(8):
                for t in range(GROUPS):
                    for jj in range(2):
                        target[which, GROUPS * s + t, 8 * jj : 8 * jj + 8, :] = FLAT[
                            t, pl.ds((rows * BAND + 8 * jj) * 8 + s, 8, stride=8), :
                        ]


def last_kernel(where_ref, sums, keep, got, increment, residual, held):
    half = pl.program_id(0) // 2

    def scalars():
        table = sums[...].T

        def total(x):
            return jnp.sum(x, axis=1, keepdims=True)

        bb, bm, mus, zz, zy, zm, by, zb = (table[j : j + 1] for j in range(8))
        rr = total(bb)
        h = total(bm)
        mu = h / rr
        off = mus - mu
        a1 = rr / (rr + h)
        z_z = total(zz + 2.0 * off * zb + off * off * bb)
        z_m = total(zm + off * bm)
        b_q = total(by + off * bm)
        z_q = total(zy + off * (zm + by) + off * off * bm)
        new = a1 * a1 * z_z
        beta = new / rr
        size = new + beta * beta * rr
        curve = size + a1 * a1 * z_q - a1 * beta * (z_m + b_q) + beta * beta * h
        for n, x in enumerate((mu, a1, new / curve, beta)):
            held[n] = jnp.broadcast_to(x, (8, LANES))

    pl.when(pl.program_id(0) == 0)(scalars)
    mu, a1, a2, beta = (held[n] for n in range(4))

    def write(ref):
        def one(i, carry):
            for c in range(8):
                for j in range(2):
                    at = (i * 8 + c, slice(8 * j, 8 * j + 8))
                    b, m, n = ref[(0,) + at], ref[(1,) + at], ref[(2,) + at]
                    r = a1 * (mu * b - m)
                    image = a1 * (mu * m - n) + beta * m
                    d = r + beta * b
                    increment[at] = a1 * b + a2 * d
                    residual[at] = r - a2 * (d + image)
            return carry

        lax.fori_loop(0, HALF // 16, one, 0)

    pl.when(half == where_ref[1])(lambda: write(keep))
    pl.when(half != where_ref[1])(lambda: write(got))


def spec(memory_space=pltpu.VMEM):
    return pl.BlockSpec(memory_space=memory_space)


def scratch():
    f32 = jnp.float32
    return [
        pltpu.VMEM(((ROWS + 1) * LINE, LANES), f32),
        pltpu.VMEM(((ROWS + 1) * LINE, LANES), f32),
        pltpu.VMEM((ROWS * LINE, LANES), f32),
        pltpu.VMEM((ROWS * LINE, LANES), f32),
        pltpu.VMEM((ROWS * LINE, LANES), f32),
        pltpu.VMEM((ROWS * STEPS, LANES), f32),
        pltpu.VMEM((5 * STEPS, ROWS, LANES), f32),
        pltpu.VMEM((3, 256, 9 * LANES), jnp.bfloat16),
        pltpu.VMEM((32 * LINE, LANES), f32),
        pltpu.VMEM((32 * LINE, LANES), f32),
        pltpu.VMEM((32 * LINE, LANES), f32),
        pltpu.SemaphoreType.DMA((3,)),
    ]


def local(
    kappa_east, kappa_north, depth, sigma, obs_precision, obs_tile, obs_col, obs_lat, innovation
):
    f32 = jnp.float32
    channels = sigma.shape[0]
    lon_tiles = lax.axis_size("lon")
    lat_tiles = lax.axis_size("lat")
    lat_here = lax.axis_index("lat")
    place = jnp.stack([lat_here // 2, lat_here % 2]).astype(jnp.int32)
    core = lat_here % 2
    params = lambda size: pltpu.CompilerParams(vmem_limit_bytes=size)

    packed = pl.pallas_call(
        lambda *refs: pack_kernel(lon_tiles, *refs),
        out_shape=jax.ShapeDtypeStruct((lon_tiles, lat_tiles, CAP, 256), f32),
        in_specs=[spec()] * 4,
        out_specs=spec(),
        scratch_shapes=[pltpu.VMEM((2 * HALF, LANES), f32)],
        compiler_params=params(VMEM_LIMIT),
        name="pack",
    )(
        obs_tile.reshape(1, LANES),
        obs_lat.reshape(1, LANES),
        obs_col.reshape(1, LANES),
        innovation,
    )
    stacked = jnp.stack([kappa_east, kappa_north, depth.astype(f32)])
    count = lon_tiles
    right = lax.ppermute(stacked[:, :, :EDGE], "lon", [((i + 1) % count, i) for i in range(count)])
    left = lax.ppermute(stacked[:, :, -EDGE:], "lon", [(i, (i + 1) % count) for i in range(count)])
    recv = lax.all_to_all(
        packed.reshape(lon_tiles * lat_tiles, CAP, 256), ALL, 0, 0, tiled=True
    ).reshape(lon_tiles, lat_tiles, CAP, 256)

    rim = jnp.concatenate([right, left, right, left], axis=2)
    geo = lax.all_gather(jnp.concatenate([stacked, rim]), "lat", axis=1, tiled=True)

    order = core * HALF + jnp.arange(HALF, dtype=jnp.int32)
    level = jnp.where(order < 2 * NZ, order % NZ, jnp.where(order < channels, 0, 1 << 20))
    pads = jnp.zeros((2 * HALF - channels,), f32)
    scale = lax.dynamic_slice_in_dim(jnp.concatenate([sigma, pads]), core * HALF, HALF)
    weight = lax.dynamic_slice_in_dim(jnp.concatenate([obs_precision, pads]), core * HALF, HALF)
    par = jnp.stack([level.astype(f32), scale * weight, scale * scale * weight])
    par = jnp.repeat(par.reshape(3, 8, GROUPS), SEGS, axis=2)
    fills = jnp.broadcast_to(jnp.array([1 << 20, 0, 0], f32)[:, None, None], (3, 8, 8))
    par = jnp.concatenate([par, fills], axis=2)

    series = jax.ShapeDtypeStruct((32 * LINE, LANES), f32)
    sb, sm, sn, sums = pl.pallas_call(
        main_kernel,
        out_shape=(
            series,
            series,
            series,
            jax.ShapeDtypeStruct((lon_tiles * lat_tiles, LANES), f32),
        ),
        in_specs=[spec(pltpu.SMEM), spec(), spec(), spec()],
        out_specs=(spec(pltpu.HBM), spec(pltpu.HBM), spec(pltpu.HBM), spec()),
        scratch_shapes=scratch(),
        compiler_params=params(VMEM_LIMIT),
        name="iterate",
    )(place, recv, geo, par)

    sums = lax.all_to_all(sums, ALL, 0, 0, tiled=True)
    tile_shape = jax.ShapeDtypeStruct((3, HALF, BAND, LANES), f32)
    keep, send = pl.pallas_call(
        spread_kernel,
        out_shape=(tile_shape, tile_shape),
        in_specs=[spec(pltpu.SMEM)] + [spec(pltpu.HBM)] * 3,
        out_specs=(spec(), spec()),
        scratch_shapes=[
            pltpu.VMEM((STEPS * LANES, GROUPS * LANES), jnp.bfloat16),
            pltpu.VMEM((256, STEPS * LANES), jnp.bfloat16),
            pltpu.VMEM((256, STEPS * LANES), jnp.bfloat16),
            pltpu.VMEM((GROUPS, 256, LANES), f32),
            pltpu.VMEM((3, 32 * LINE, LANES), f32),
            pltpu.SemaphoreType.DMA((3,)),
        ],
        compiler_params=params(VMEM_LIMIT),
        cost_estimate=pl.CostEstimate(flops=8_000_000_000, bytes_accessed=10_000_000, transcendentals=0),
        name="spread",
    )(place, sb, sm, sn)
    send, sums = lax.optimization_barrier((send, sums))
    got = lax.ppermute(send, "lat", [(i, i ^ 1) for i in range(lat_tiles)])
    out = jax.ShapeDtypeStruct((channels, BAND, LANES), f32)
    early = lambda i: jnp.minimum(i, 1)
    late = lambda i: jnp.maximum(i - 2, 0)
    block = (3, HALF // 2, BAND, LANES)
    return pl.pallas_call(
        last_kernel,
        out_shape=(out, out),
        grid_spec=pltpu.PrefetchScalarGridSpec(
            num_scalar_prefetch=1,
            grid=(4,),
            in_specs=[
                pl.BlockSpec((lon_tiles * lat_tiles, LANES), lambda i, w: (0, 0)),
                pl.BlockSpec(block, lambda i, w: (0, jnp.where(w[1] == 0, early(i), late(i)), 0, 0)),
                pl.BlockSpec(block, lambda i, w: (0, jnp.where(w[1] == 0, late(i), early(i)), 0, 0)),
            ],
            out_specs=(
                pl.BlockSpec((HALF // 2, BAND, LANES), lambda i, w: (i, 0, 0)),
                pl.BlockSpec((HALF // 2, BAND, LANES), lambda i, w: (i, 0, 0)),
            ),
            scratch_shapes=[pltpu.VMEM((4, 8, LANES), f32)],
        ),
        compiler_params=params(16 * MIB),
        name="combine",
    )(place, sums, keep, got)


def solution(mesh):
    return jax.shard_map(
        local,
        mesh=mesh,
        in_specs=(
            P("lat", "lon"),
            P("lat", "lon"),
            P("lat", "lon"),
            P(),
            P(),
            P(("lon", "lat"), None),
            P(("lon", "lat")),
            P(("lon", "lat")),
            P(None, ("lon", "lat")),
        ),
        out_specs=(P(None, "lat", "lon"), P(None, "lat", "lon")),
        check_vma=False,
    )
```
